512 devices in a mesh: group: 8 (over y, core), slot: 16 (over z), ctx: 4 (over x).
Axes of the slice: x: 4, y: 4, z: 16, core: 2. Of those that a mesh axis runs over, the one named last changes fastest.
Arguments:
- queries: bfloat16 [8, 16, 512, 4096], P('group', 'slot', 'ctx'), may hold values from -0.5 to 0.5
- keys: bfloat16 [8, 16, 512, 4096], P('group', 'slot', 'ctx'), may hold values from -0.5 to 0.5
- values: bfloat16 [8, 16, 512, 4096], P('group', 'slot', 'ctx'), may hold values from -6 to 6
- lengths: int32 [8, 16], P('group', 'slot'), may hold values from 1 to 512
- rewards: float32 [8, 16], P('group', 'slot'), may hold values from 0 to 4
- decay_rate: float32 [32], replicated, may hold values from 0.0002 to 0.03
- prompt_state: float32 [8, 4096, 128], P('group', ('slot', 'ctx')), may hold values from -6 to 6
Outputs:
- key_grad: bfloat16 [8, 16, 512, 4096], P('group', 'slot', 'ctx')
- prompt_grad: float32 [8, 4096, 128], P('group', ('slot', 'ctx'))
The draws below stay inside these ranges and needn't reach their ends.
All inputs are finite; a program needn't handle non-finite values.
Results may differ from the reference program's by a relative error of at most 0.0039.
Values sent between devices are 32-bit elements; how exact they have to be, the bound alone decides.
No kernel may reach another device: no remote copies, remote signals or barrier semaphores. Data moves between devices by JAX's collectives and lax.ppermute only.
A program may use at most 64 MiB of HBM per device.

```python
import math
import jax
import jax.numpy as jnp
from jax import lax

HEADS = 32
HDIM = 128
TOK_DEV = 128
PROMPTS = 8
RESPONSES = 16
WINDOW = 512


def touch_ends(drawn, key, smallest, high):
    place = [jax.random.randint(jax.random.fold_in(key, axis), (), 0, length) for axis, length in enumerate(drawn.shape)]
    widest = drawn.shape.index(max(drawn.shape))
    neighbour = place[:widest] + [(place[widest] + 1) % drawn.shape[widest]] + place[widest + 1:]
    return drawn.at[tuple(place)].set(smallest).at[tuple(neighbour)].set(high)


def shard_levels(stream_key, dims, pieces, least, high):
    def one(axis_at, shards_of):
        draws = jax.random.uniform(jax.random.fold_in(jax.random.fold_in(stream_key, 6), axis_at), (shards_of,), jnp.float32, least / len(pieces), high / len(pieces))
        return jnp.repeat(jnp.exp(draws), dims[axis_at] // shards_of).reshape((-1,) + (1,) * (len(dims) - axis_at - 1))

    loudness = one(*pieces[0])
    for cut in pieces[1:]:
        loudness = loudness * one(*cut)
    return loudness


def bell_draw(stream_key, extent, spread, bound, split=(), kind=jnp.bfloat16):
    factor_of = shard_levels(stream_key, extent, split, -0.22, 0.18) if split else 1.0
    drawn = jax.random.normal(stream_key, extent, jnp.float32) * spread * factor_of
    return jnp.minimum(jnp.maximum(drawn, -bound), bound).astype(kind)


def setup_inputs(seed: int = 0) -> dict:
    key_list = jax.random.split(jax.random.key(seed), 8)
    return {
        "queries": bell_draw(key_list[0], (PROMPTS, RESPONSES, WINDOW, HEADS * HDIM), HDIM ** -0.5, 0.5, ((0, 8), (1, 16), (2, 4))),
        "keys": bell_draw(key_list[1], (PROMPTS, RESPONSES, WINDOW, HEADS * HDIM), HDIM ** -0.5, 0.5, ((0, 8), (1, 16), (2, 4))),
        "values": bell_draw(key_list[2], (PROMPTS, RESPONSES, WINDOW, HEADS * HDIM), 1.0, 6.0, ((0, 8), (1, 16), (2, 4))),
        "lengths": touch_ends(jax.random.randint(key_list[3], (PROMPTS, RESPONSES), 1, WINDOW + 1), jax.random.fold_in(key_list[3], 1), 1, WINDOW).astype(jnp.int32),
        "rewards": jnp.clip(4.0 * jax.random.uniform(key_list[4], (PROMPTS, RESPONSES), jnp.float32) ** shard_levels(key_list[4], (PROMPTS, RESPONSES), ((0, 8), (1, 16)), -0.2, 0.2), 0.0, 4.0),
        "decay_rate": jnp.clip(jnp.exp(jax.random.uniform(key_list[5], (HEADS,), jnp.float32, math.log(0.0002), math.log(0.03))), 0.0002, 0.03),
        "prompt_state": bell_draw(key_list[6], (PROMPTS, HEADS * HDIM, HDIM), 1.0, 6.0, ((0, 8), (1, 64)), jnp.float32),
    }


loss_scale = 16.0
highest = lax.Precision.HIGHEST


def round_within(raw, same_block):
    rounded = lax.optimization_barrier(raw.astype(jnp.bfloat16)).astype(jnp.float32)
    return jnp.where(same_block[None], rounded, raw)


def response_grads(query_rows, key_rows, value_rows, length, factor, prompt, decay_rate):
    positions = jnp.arange(WINDOW, dtype=jnp.int32)
    keep_mask = (positions < length).astype(jnp.float32)
    block_ids = positions // TOK_DEV
    same_block = block_ids[:, None] == block_ids[None, :]
    query_f = query_rows.astype(jnp.float32).reshape(WINDOW, HEADS, HDIM)
    key_f = key_rows.astype(jnp.float32).reshape(WINDOW, HEADS, HDIM) * keep_mask[:, None, None]
    value_f = value_rows.astype(jnp.float32).reshape(WINDOW, HEADS, HDIM) * keep_mask[:, None, None]
    place_f = jnp.arange(WINDOW, dtype=jnp.float32)
    offset = place_f[:, None] - place_f[None, :]
    decay_grid = jnp.where(offset[None] >= 0.0, jnp.exp(-decay_rate[:, None, None] * jnp.maximum(offset, 0.0)[None]), 0.0)
    scores = jnp.einsum('phd,shd->hps', query_f, key_f, precision=highest) * decay_grid
    scores = round_within(scores, same_block)
    inward = jnp.exp(-(place_f[:, None] + 1.0) * decay_rate[None, :])
    output = jnp.einsum('hps,shd->phd', scores, value_f, precision=highest)
    output = output + inward[:, :, None] * jnp.einsum('phd,hde->phe', query_f, prompt, precision=highest)
    cotangent = ((factor * keep_mask)[:, None, None] * output).astype(jnp.bfloat16).astype(jnp.float32)
    weights = jnp.einsum('phe,she->hps', cotangent, value_f, precision=highest) * decay_grid
    weights = round_within(weights, same_block)
    key_grads = keep_mask[:, None, None] * jnp.einsum('hps,phd->shd', weights, query_f, precision=highest)
    prompt_term = jnp.einsum('phd,phe->hde', query_f * inward[:, :, None], cotangent, precision=highest)
    return key_grads.astype(jnp.bfloat16).reshape(WINDOW, HEADS * HDIM), prompt_term


def reference(queries, keys, values, lengths, rewards, decay_rate, prompt_state):
    token_total = jnp.sum(lengths.astype(jnp.float32))
    advantage = rewards - jnp.mean(rewards, axis=1, keepdims=True)
    factors = loss_scale * advantage * (PROMPTS * RESPONSES) / token_total

    def per_prompt(prompt_index):
        prompt = prompt_state[prompt_index].reshape(HEADS, HDIM, HDIM)

        def per_response(running, slot_index):
            key_grads, prompt_term = response_grads(queries[prompt_index, slot_index], keys[prompt_index, slot_index], values[prompt_index, slot_index], lengths[prompt_index, slot_index], factors[prompt_index, slot_index], prompt, decay_rate)
            return running + prompt_term, key_grads

        summed, key_grads = lax.scan(per_response, jnp.zeros((HEADS, HDIM, HDIM), jnp.float32), jnp.arange(RESPONSES, dtype=jnp.int32))
        return key_grads, summed.reshape(HEADS * HDIM, HDIM)

    key_grad, prompt_grad = lax.map(per_prompt, jnp.arange(PROMPTS, dtype=jnp.int32))
    return key_grad, prompt_grad
```

```python
import functools

import jax
import jax.numpy as jnp
from jax import lax
from jax.experimental import pallas as pl
from jax.experimental.pallas import tpu as pltpu
from jax.sharding import PartitionSpec as P

loss_scale = 16.0
f32 = jnp.float32
bf16 = jnp.bfloat16
chunk_heads = (4, 4)
lane = 128
vmem_bytes = 40 * 1024 * 1024


def dot(a, b, dims):
    return lax.dot_general(a, b, ((dims[0], dims[1]), ((), ())), preferred_element_type=f32)


def halves(x):
    hi = x.astype(bf16)
    return hi, (x - hi.astype(f32)).astype(bf16)


def pack_body(place, *refs):
    sources, sends = refs[:9], refs[9:]
    for turn in range(3):
        for which in range(3):
            sends[turn][which, 0] = sources[3 * turn + which][...].astype(f32)


def pack(place, arrays, block_len, start, count):
    def column(turn):
        return lambda m, place: (0, lax.rem(place[0] + turn, 4) + 4 * (start + m))

    in_specs = [
        pl.BlockSpec((block_len, lane), column(turn)) for turn in (1, 2, 3) for _ in arrays
    ]
    shape = (3, count, block_len, lane)
    return pl.pallas_call(
        pack_body,
        grid_spec=pltpu.PrefetchScalarGridSpec(
            num_scalar_prefetch=1,
            grid=(count,),
            in_specs=in_specs,
            out_specs=[
                pl.BlockSpec((3, 1, block_len, lane), lambda m, place: (0, m, 0, 0))
            ]
            * 3,
        ),
        out_shape=[jax.ShapeDtypeStruct(shape, f32)] * 3,
        compiler_params=pltpu.CompilerParams(vmem_limit_bytes=vmem_bytes),
        cost_estimate=pl.CostEstimate(
            flops=0, bytes_accessed=18 * count * block_len * lane * 3 // 3, transcendentals=0
        ),
    )(place, *(list(arrays) * 3))


def main_body(start, place, rates, factor_ref, *refs):
    local, moved, prompt_ref = refs[:3], refs[3:6], refs[6]
    refs = refs[7:] if start == 0 else refs[8:]
    outs, prompt_grad_ref = refs[:4], refs[4]
    rows_q, rows_k, rows_v, grads = refs[5:]
    me, length = place[0], place[1]
    factor = factor_ref[0]
    rate = rates[me + 4 * (start + pl.program_id(0))]
    row = lax.broadcasted_iota(jnp.int32, (lane, lane), 0)
    col = lax.broadcasted_iota(jnp.int32, (lane, lane), 1)
    row_f, offset = row.astype(f32), (row - col).astype(f32)
    decay = jnp.where(offset >= 0.0, jnp.exp(-rate * jnp.maximum(offset, 0.0)), 0.0)
    inward = jnp.exp(-(row_f + 1.0) * rate)
    outward = jnp.exp(-(lane - 1.0 - row_f) * rate)
    block_decay = jnp.exp(jnp.full((lane, lane), -float(lane), f32) * rate)

    def live(block):
        return (row + lane * block < length).astype(f32)

    for turn in range(4):
        block = lax.rem(me + 4 - turn, 4)
        if turn == 0:
            q, k, v = (r[...].astype(f32) for r in local)
        else:
            q, k, v = (moved[turn - 1][which, 0] for which in range(3))
        keep = live(block)
        rows_q[block] = q.astype(bf16)
        rows_k[block] = (k * keep).astype(bf16)
        rows_v[block] = (v * keep).astype(bf16)

    state = jnp.concatenate([prompt_ref[0, :64], prompt_ref[1, :64]], 0)
    cotangents = []
    for block in range(4):
        q, k, v = rows_q[block], rows_k[block], rows_v[block]
        scores = (dot(q, k, ((1,), (1,))) * decay).astype(bf16)
        state_hi, state_lo = halves(state)
        carried = dot(q, state_hi, ((1,), (0,))) + dot(q, state_lo, ((1,), (0,)))
        output = dot(scores, v, ((1,), (0,))) + inward * carried
        cotangents.append((factor * live(block) * output).astype(bf16))
        if block < 3:
            k_hi, k_lo = halves(k.astype(f32) * outward)
            state = block_decay * state + dot(k_hi, v, ((0,), (0,))) + dot(k_lo, v, ((0,), (0,)))
    state = None
    for block in (3, 2, 1, 0):
        q, v, cotangent = rows_q[block], rows_v[block], cotangents[block]
        weights = (dot(cotangent, v, ((1,), (1,))) * decay).astype(bf16)
        grad = dot(weights, q, ((0,), (0,)))
        q_hi, q_lo = halves(q.astype(f32) * inward)
        gained = dot(q_hi, cotangent, ((0,), (0,))) + dot(q_lo, cotangent, ((0,), (0,)))
        if state is None:
            state = gained
        else:
            state_hi, state_lo = halves(state)
            carried = dot(v, state_hi, ((1,), (1,))) + dot(v, state_lo, ((1,), (1,)))
            grad = grad + outward * carried
            state = block_decay * state + gained
        grads[block] = live(block) * grad
    prompt_grad_ref[0] = state
    for turn in range(4):
        outs[turn][0] = grads[lax.rem(me + turn, 4)]


def main(place, rates, factor, arrays, moved, prompt, so_far, block_len, start, count):
    assert block_len == lane
    head_block = lambda m, place: (0, place[0] + 4 * (start + m))
    in_specs = [
        pl.BlockSpec(memory_space=pltpu.SMEM),
        pl.BlockSpec(memory_space=pltpu.SMEM),
    ]
    in_specs += [pl.BlockSpec((block_len, lane), head_block)] * 3
    in_specs += [pl.BlockSpec((3, 1, block_len, lane), lambda m, place: (0, m, 0, 0))] * 3
    in_specs += [pl.BlockSpec((2,) + prompt.shape[1:], lambda m, place: (start + m, 0, 0))]
    args = [place, rates, factor, *arrays, *moved, prompt]
    aliases = {}
    if so_far is not None:
        in_specs.append(pl.BlockSpec(memory_space=pl.ANY))
        aliases = {len(args): 4}
        args.append(so_far)
    one = pl.BlockSpec((1, block_len, lane), lambda m, place: (m, 0, 0))
    return pl.pallas_call(
        functools.partial(main_body, start),
        grid_spec=pltpu.PrefetchScalarGridSpec(
            num_scalar_prefetch=1,
            grid=(count,),
            in_specs=in_specs,
            out_specs=[one] * 4
            + [pl.BlockSpec((1, lane, lane), lambda m, place: (start + m, 0, 0))],
            scratch_shapes=[pltpu.VMEM((4, lane, lane), bf16)] * 3
            + [pltpu.VMEM((4, lane, lane), f32)],
        ),
        out_shape=[jax.ShapeDtypeStruct((count, block_len, lane), f32)] * 4
        + [jax.ShapeDtypeStruct((8, lane, lane), f32)],
        input_output_aliases=aliases,
        compiler_params=pltpu.CompilerParams(vmem_limit_bytes=vmem_bytes),
        cost_estimate=pl.CostEstimate(
            flops=count * 4 * 15 * 2 * lane**3,
            bytes_accessed=count * lane * lane * 4 * 20,
            transcendentals=0,
        ),
    )(*args)


def place_body(start, place, *refs):
    parts, out = refs[:4], refs[-1]
    for turn in range(4):
        owner = lax.rem(place[0] + 4 - turn, 4)
        out[:, pl.ds(pl.multiple_of(owner * lane, lane), lane)] = parts[turn][0].astype(bf16)


def put(place, parts, so_far, block_len, start, count, width):
    in_specs = [pl.BlockSpec((1, block_len, lane), lambda m, place: (m, 0, 0))] * 4
    args = [place, *parts]
    aliases = {}
    if so_far is not None:
        in_specs.append(pl.BlockSpec(memory_space=pl.ANY))
        aliases = {len(args): 0}
        args.append(so_far)
    return pl.pallas_call(
        functools.partial(place_body, start),
        grid_spec=pltpu.PrefetchScalarGridSpec(
            num_scalar_prefetch=1,
            grid=(count,),
            in_specs=in_specs,
            out_specs=pl.BlockSpec((block_len, 4 * lane), lambda m, place: (0, start + m)),
        ),
        out_shape=jax.ShapeDtypeStruct((block_len, width), bf16),
        input_output_aliases=aliases,
        compiler_params=pltpu.CompilerParams(vmem_limit_bytes=vmem_bytes),
        cost_estimate=pl.CostEstimate(
            flops=0, bytes_accessed=count * block_len * lane * 24, transcendentals=0
        ),
    )(*args)


def piece_moves():
    moves = []
    for ctx in range(4):
        for slot in range(16):
            home = 4 * (2 * (slot // 2) + ctx // 2) + 2 * (ctx % 2) + slot % 2
            moves.append((home, 4 * slot + ctx))
    return moves


def shards(queries, keys, values, lengths, rewards, decay_rate, prompt_state):
    block_len, width = queries.shape[2], queries.shape[3]
    arrays = [a.reshape(block_len, width) for a in (queries, keys, values)]
    ctx_index = lax.axis_index("ctx").astype(jnp.int32)
    length, reward = lengths[0, 0], rewards[0, 0]
    place = jnp.stack([ctx_index, length])
    moves = piece_moves()

    piece = lax.ppermute(prompt_state[0], ("slot", "ctx"), moves)
    by_group = lax.all_gather(jnp.full((8, lane), length.astype(f32)), "group", tiled=True)
    slot_tokens = jnp.sum(by_group.reshape(-1, 8, lane)[:, 0], 0, keepdims=True)
    scalars = jnp.concatenate(
        [slot_tokens, jnp.full((1, lane), reward), jnp.zeros((6, lane), f32)], 0
    )
    prompt = lax.all_gather(jnp.concatenate([piece, scalars], 0), "slot")
    rows = piece.shape[0]
    token_total = jnp.sum(prompt[:, rows, 0])
    reward_total = jnp.sum(prompt[:, rows + 1, 0])
    slots, groups = lax.axis_size("slot"), lax.axis_size("group")
    advantage = reward - reward_total / slots
    factor = (loss_scale * advantage * (groups * slots) / token_total).reshape(1)

    starts = [sum(chunk_heads[:n]) for n in range(len(chunk_heads))]
    rings = [[(i, (i + turn) % 4) for i in range(4)] for turn in range(4)]

    def turned(parts):
        return [lax.ppermute(parts[turn - 1], "ctx", rings[turn]) for turn in (1, 2, 3)]

    moved = [
        turned(pack(place, arrays, block_len, start, count))
        for start, count in zip(starts, chunk_heads)
    ]
    prompt_grad, key_parts = None, []
    for start, count, parts in zip(starts, chunk_heads, moved):
        *out, prompt_grad = main(
            place, decay_rate, factor, arrays, parts, prompt, prompt_grad, block_len, start, count
        )
        key_parts.append([out[0], *turned(out[1:])])
    summed = lax.psum_scatter(prompt_grad.reshape(-1, rows, lane), "slot", tiled=True)
    summed = lax.ppermute(summed, ("slot", "ctx"), [(there, home) for home, there in moves])
    key_grad = None
    for start, count, parts in zip(starts, chunk_heads, key_parts):
        key_grad = put(place, parts, key_grad, block_len, start, count, width)
    return (key_grad.reshape(1, 1, block_len, width), summed)


def solution(mesh):
    placed = (
        P("group", "slot", "ctx", None),
        P("group", "slot", "ctx", None),
        P("group", "slot", "ctx", None),
        P("group", "slot"),
        P("group", "slot"),
        P(),
        P("group", ("slot", "ctx"), None),
    )
    return jax.shard_map(
        shards,
        mesh=mesh,
        in_specs=placed,
        out_specs=(P("group", "slot", "ctx", None), P("group", ("slot", "ctx"), None)),
        check_vma=False,
    )
```

```python
import functools

import jax
import jax.numpy as jnp
from jax import lax
from jax.experimental import pallas as pl
from jax.experimental.pallas import tpu as pltpu
from jax.sharding import PartitionSpec as P

loss_scale = 16.0
f32 = jnp.float32
bf16 = jnp.bfloat16
chunk_heads = (8,)
lane = 128


def dot(a, b, dims):
    return lax.dot_general(a, b, ((dims[0], dims[1]), ((), ())), preferred_element_type=f32)


def halves(x):
    hi = x.astype(bf16)
    return hi, (x - hi.astype(f32)).astype(bf16)


def pack_body(heads, place, *refs):
    sources, sends = refs[:3], refs[3:]
    for turn in range(3):
        owner = lax.rem(place[0] + turn + 1, 4)
        for which in range(3):
            for step in range(heads):
                column = pl.multiple_of((owner + 4 * step) * lane, lane)
                sends[turn][which, step] = sources[which][:, pl.ds(column, lane)].astype(f32)


def pack(place, arrays, block_len, start, count, heads=4):
    first = start // heads
    return pl.pallas_call(
        functools.partial(pack_body, heads),
        grid_spec=pltpu.PrefetchScalarGridSpec(
            num_scalar_prefetch=1,
            grid=(count // heads,),
            in_specs=[
                pl.BlockSpec((block_len, 4 * heads * lane), lambda m, place: (0, first + m))
            ]
            * 3,
            out_specs=[
                pl.BlockSpec((3, heads, block_len, lane), lambda m, place: (0, m, 0, 0))
            ]
            * 3,
        ),
        out_shape=[jax.ShapeDtypeStruct((3, count, block_len, lane), f32)] * 3,
        cost_estimate=pl.CostEstimate(
            flops=0, bytes_accessed=60 * count * block_len * lane, transcendentals=0
        ),
    )(place, *arrays)


def head_grads(rates, factor, length, rows, states):
    row = lax.broadcasted_iota(jnp.int32, (lane, lane), 0)
    col = lax.broadcasted_iota(jnp.int32, (lane, lane), 1)
    row_f, offset = row.astype(f32), (row - col).astype(f32)
    keep = [(row + lane * block < length).astype(f32) for block in range(4)]
    heads = range(len(rates))
    decay = [
        jnp.where(offset >= 0.0, jnp.exp(-rate * jnp.maximum(offset, 0.0)), 0.0) for rate in rates
    ]
    inward = [jnp.exp(-(row_f + 1.0) * rate) for rate in rates]
    outward = [jnp.exp(-(lane - 1.0 - row_f) * rate) for rate in rates]
    block_decay = [jnp.exp(jnp.full((lane, lane), -float(lane), f32) * rate) for rate in rates]
    q, k, v = ({(h, b): rows[h][n][b] for h in heads for b in range(4)} for n in range(3))
    forward = [(h, b) for b in range(4) for h in heads]
    backward = forward[::-1]

    def two(a, b, dims):
        a, b = jnp.concatenate(a, dims[0][0]), jnp.concatenate(b, dims[1][0])
        return dot(a, b, dims)

    scores, gained, states_at = {}, {}, {}
    for at in forward:
        scores[at] = (dot(q[at], k[at], ((1,), (1,))) * decay[at[0]]).astype(bf16)
    for at in forward:
        if at[1] < 3:
            scaled = halves(k[at].astype(f32) * outward[at[0]])
            gained[at] = two(scaled, (v[at], v[at]), ((0,), (0,)))
    for h in heads:
        state = states[h]
        for b in range(4):
            states_at[h, b] = halves(state)
            if b < 3:
                state = block_decay[h] * state + gained[h, b]
    cotangents = {}
    for at in forward:
        carried = two((q[at], q[at]), states_at[at], ((1,), (0,)))
        output = dot(scores[at], v[at], ((1,), (0,))) + inward[at[0]] * carried
        cotangents[at] = (factor * keep[at[1]] * output).astype(bf16)
    for at in backward:
        scaled = halves(q[at].astype(f32) * inward[at[0]])
        gained[at] = two(scaled, (cotangents[at], cotangents[at]), ((0,), (0,)))
    ends = []
    for h in heads:
        state = gained[h, 3]
        for b in (2, 1, 0):
            states_at[h, b] = halves(state)
            state = block_decay[h] * state + gained[h, b]
        ends.append(state)
    weights, grads = {}, {}
    for at in backward:
        weights[at] = (dot(cotangents[at], v[at], ((1,), (1,))) * decay[at[0]]).astype(bf16)
    for at in backward:
        grad = dot(weights[at], q[at], ((0,), (0,)))
        if at[1] < 3:
            carried = two((v[at], v[at]), states_at[at], ((1,), (1,)))
            grad = grad + outward[at[0]] * carried
        grads[at] = keep[at[1]] * grad
    return grads, ends


def main_body(start, heads, aliased, place, rates, factor_ref, *refs):
    local, moved, prompt_ref = refs[:3], refs[3:6], refs[6]
    refs = refs[7 + aliased :]
    outs, prompt_grad_ref = refs[:4], refs[4]
    rows_q, rows_k, rows_v, grads_ref = refs[5:]
    me, length = place[0], place[1]
    row = lax.broadcasted_iota(jnp.int32, (lane, lane), 0)
    for step in range(heads):
        for turn in range(4):
            block = lax.rem(me + 4 - turn, 4)
            if turn == 0:
                column = pl.ds(pl.multiple_of((me + 4 * step) * lane, lane), lane)
                q, k, v = (r[:, column].astype(f32) for r in local)
            else:
                q, k, v = (moved[turn - 1][which, step] for which in range(3))
            keep = (row + lane * block < length).astype(f32)
            rows_q[step, block] = q.astype(bf16)
            rows_k[step, block] = (k * keep).astype(bf16)
            rows_v[step, block] = (v * keep).astype(bf16)
    half, steps = lane // 2, range(heads)
    head = me + 4 * (start + pl.program_id(0) * heads)
    prompts = [
        jnp.concatenate([prompt_ref[2 * step, :half], prompt_ref[2 * step + 1, :half]], 0)
        for step in steps
    ]
    rows = [
        [[r[step, block] for block in range(4)] for r in (rows_q, rows_k, rows_v)]
        for step in steps
    ]
    grads, ends = head_grads(
        [rates[head + 4 * step] for step in steps], factor_ref[0], length, rows, prompts
    )
    for step in steps:
        for block in range(4):
            grads_ref[step, block] = grads[step, block]
        prompt_grad_ref[step] = ends[step]
    for step in range(heads):
        for turn in range(4):
            outs[turn][step] = grads_ref[step, lax.rem(me + turn, 4)]


def main(place, rates, factor, arrays, moved, prompt, so_far, block_len, start, count, heads=2):
    assert block_len == lane
    first, total = start // heads, prompt.shape[0] // 2
    in_specs = [pl.BlockSpec(memory_space=pltpu.SMEM)] * 2
    in_specs += [
        pl.BlockSpec((block_len, 4 * heads * lane), lambda m, place: (0, first + m))
    ] * 3
    in_specs += [pl.BlockSpec((3, heads, block_len, lane), lambda m, place: (0, m, 0, 0))] * 3
    in_specs += [
        pl.BlockSpec((2 * heads,) + prompt.shape[1:], lambda m, place: (first + m, 0, 0))
    ]
    args = [place, rates, factor, *arrays, *moved, prompt]
    aliases = {len(args) + n: n for n in range(len(so_far))}
    in_specs += [pl.BlockSpec(memory_space=pl.ANY)] * len(so_far)
    one = pl.BlockSpec((heads, block_len, lane), lambda m, place: (first + m, 0, 0))
    return pl.pallas_call(
        functools.partial(main_body, start, heads, len(so_far)),
        grid_spec=pltpu.PrefetchScalarGridSpec(
            num_scalar_prefetch=1,
            grid=(count // heads,),
            in_specs=in_specs,
            out_specs=[one] * 5,
            scratch_shapes=[pltpu.VMEM((heads, 4, lane, lane), bf16)] * 3
            + [pltpu.VMEM((heads, 4, lane, lane), f32)],
        ),
        out_shape=[jax.ShapeDtypeStruct((total, block_len, lane), f32)] * 5,
        input_output_aliases=aliases,
        cost_estimate=pl.CostEstimate(
            flops=count * 4 * 15 * 2 * lane**3,
            bytes_accessed=count * lane * lane * 4 * 20,
            transcendentals=0,
        ),
    )(*args, *so_far)


def put_body(heads, place, *refs):
    parts, out = refs[:4], refs[4]
    for turn in range(4):
        owner = lax.rem(place[0] + 4 - turn, 4)
        for step in range(heads):
            column = pl.multiple_of((owner + 4 * step) * lane, lane)
            out[:, pl.ds(column, lane)] = parts[turn][step].astype(bf16)


def put(place, parts, block_len, width, heads=4):
    return pl.pallas_call(
        functools.partial(put_body, heads),
        grid_spec=pltpu.PrefetchScalarGridSpec(
            num_scalar_prefetch=1,
            grid=(parts[0].shape[0] // heads,),
            in_specs=[pl.BlockSpec((heads, block_len, lane), lambda m, place: (m, 0, 0))] * 4,
            out_specs=pl.BlockSpec((block_len, 4 * heads * lane), lambda m, place: (0, m)),
        ),
        out_shape=jax.ShapeDtypeStruct((block_len, width), bf16),
        cost_estimate=pl.CostEstimate(
            flops=0, bytes_accessed=parts[0].size * 24, transcendentals=0
        ),
    )(place, *parts)


def piece_moves():
    moves = []
    for ctx in range(4):
        for slot in range(16):
            home = 4 * (2 * (slot // 2) + ctx // 2) + 2 * (ctx % 2) + slot % 2
            moves.append((home, 4 * slot + ctx))
    return moves


def shards(queries, keys, values, lengths, rewards, decay_rate, prompt_state):
    block_len, width = queries.shape[2], queries.shape[3]
    arrays = [a.reshape(block_len, width) for a in (queries, keys, values)]
    ctx_index = lax.axis_index("ctx").astype(jnp.int32)
    length, reward = lengths[0, 0], rewards[0, 0]
    place = jnp.stack([ctx_index, length])
    moves = piece_moves()

    piece = lax.ppermute(prompt_state[0], ("slot", "ctx"), moves)
    rings = [[(i, (i + turn) % 4) for i in range(4)] for turn in range(4)]
    starts = [sum(chunk_heads[:n]) for n in range(len(chunk_heads))]

    def turned(parts):
        return [lax.ppermute(parts[turn - 1], "ctx", rings[turn]) for turn in (1, 2, 3)]

    sends = [
        pack(place, arrays, block_len, start, count) for start, count in zip(starts, chunk_heads)
    ]
    piece, sends = lax.optimization_barrier((piece, sends))
    moved = [turned(parts) for parts in sends]

    by_group = lax.all_gather(jnp.full((8, lane), length.astype(f32)), "group", tiled=True)
    slot_tokens = jnp.sum(by_group.reshape(-1, 8, lane)[:, 0], 0, keepdims=True)
    scalars = jnp.concatenate(
        [slot_tokens, jnp.full((1, lane), reward), jnp.zeros((6, lane), f32)], 0
    )
    prompt = lax.all_gather(jnp.concatenate([piece, scalars], 0), "slot")
    rows = piece.shape[0]
    token_total = jnp.sum(prompt[:, rows, 0])
    reward_total = jnp.sum(prompt[:, rows + 1, 0])
    slots, groups = lax.axis_size("slot"), lax.axis_size("group")
    advantage = reward - reward_total / slots
    factor = (loss_scale * advantage * (groups * slots) / token_total).reshape(1)

    out = ()
    for start, count, parts in zip(starts, chunk_heads, moved):
        out = main(
            place, decay_rate, factor, arrays, parts, prompt, out, block_len, start, count
        )
    back = turned(out[1:4])
    terms = lax.all_to_all(out[4].reshape(slots, rows, lane), "slot", 0, 0, tiled=True)
    summed = jnp.sum(terms, 0, keepdims=True)
    summed = lax.ppermute(summed, ("slot", "ctx"), [(there, home) for home, there in moves])
    key_grad = put(place, [out[0], *back], block_len, width)
    return (key_grad.reshape(1, 1, block_len, width), summed)


def solution(mesh):
    placed = (
        P("group", "slot", "ctx", None),
        P("group", "slot", "ctx", None),
        P("group", "slot", "ctx", None),
        P("group", "slot"),
        P("group", "slot"),
        P(),
        P("group", ("slot", "ctx"), None),
    )
    return jax.shard_map(
        shards,
        mesh=mesh,
        in_specs=placed,
        out_specs=(P("group", "slot", "ctx", None), P("group", ("slot", "ctx"), None)),
        check_vma=False,
    )
```

```python
import functools

import jax
import jax.numpy as jnp
from jax import lax
from jax.experimental import pallas as pl
from jax.experimental.pallas import tpu as pltpu
from jax.sharding import PartitionSpec as P

loss_scale = 16.0
f32 = jnp.float32
bf16 = jnp.bfloat16
early, late = 6, 2
lane = 128


def dot(a, b, dims):
    return lax.dot_general(a, b, ((dims[0], dims[1]), ((), ())), preferred_element_type=f32)


def halves(x):
    hi = x.astype(bf16)
    return hi, (x - hi.astype(f32)).astype(bf16)


def residue(device):
    return 2 * lax.rem(device, 2) + lax.div(device, 2)


def pack_body(heads, *refs):
    sources, across, soon, later = refs[:3], refs[3], refs[4:6], refs[6:8]

    def move(turn, send):
        owner = residue(lax.rem(lax.axis_index("ctx") + turn, 4))
        for which in range(3):
            for step in range(heads):
                column = pl.multiple_of((owner + 4 * step) * lane, lane)
                send[which, step] = sources[which][:, pl.ds(column, lane)].astype(f32)

    move(2, across)

    @pl.when(pl.program_id(0) < early // heads)
    def _():
        move(1, soon[0])
        move(3, soon[1])

    @pl.when(pl.program_id(0) >= early // heads)
    def _():
        move(1, later[0])
        move(3, later[1])


def pack(arrays, block_len, heads=2):
    turns = early // heads
    block = (3, heads, block_len, lane)
    soon = pl.BlockSpec(block, lambda m: (0, lax.min(m, turns - 1), 0, 0))
    later = pl.BlockSpec(block, lambda m: (0, lax.max(m - turns, 0), 0, 0))
    counts = (early + late, early, early, late, late)
    return pl.pallas_call(
        functools.partial(pack_body, heads),
        grid=((early + late) // heads,),
        in_specs=[pl.BlockSpec((block_len, 4 * heads * lane), lambda m: (0, m))] * 3,
        out_specs=[pl.BlockSpec(block, lambda m: (0, m, 0, 0)), soon, soon, later, later],
        out_shape=[jax.ShapeDtypeStruct((3, count, block_len, lane), f32) for count in counts],
        cost_estimate=pl.CostEstimate(
            flops=0, bytes_accessed=60 * (early + late) * block_len * lane, transcendentals=0
        ),
    )(*arrays)


def head_grads(rates, factor, length, rows, states):
    row = lax.broadcasted_iota(jnp.int32, (lane, lane), 0)
    col = lax.broadcasted_iota(jnp.int32, (lane, lane), 1)
    row_f, offset = row.astype(f32), (row - col).astype(f32)
    keep = [(row + lane * block < length).astype(f32) for block in range(4)]
    heads = range(len(rates))
    decay = [
        jnp.where(offset >= 0.0, jnp.exp(-rate * jnp.maximum(offset, 0.0)), 0.0) for rate in rates
    ]
    inward = [jnp.exp(-(row_f + 1.0) * rate) for rate in rates]
    outward = [jnp.exp(-(lane - 1.0 - row_f) * rate) for rate in rates]
    block_decay = [jnp.exp(jnp.full((lane, lane), -float(lane), f32) * rate) for rate in rates]
    q, k, v = ({(h, b): rows[h][n][b] for h in heads for b in range(4)} for n in range(3))
    forward = [(h, b) for b in range(4) for h in heads]
    backward = forward[::-1]

    def two(a, b, dims):
        a, b = jnp.concatenate(a, dims[0][0]), jnp.concatenate(b, dims[1][0])
        return dot(a, b, dims)

    scores, gained, states_at = {}, {}, {}
    for at in forward:
        scores[at] = (dot(q[at], k[at], ((1,), (1,))) * decay[at[0]]).astype(bf16)
    for at in forward:
        if at[1] < 3:
            scaled = halves(k[at].astype(f32) * outward[at[0]])
            gained[at] = two(scaled, (v[at], v[at]), ((0,), (0,)))
    for h in heads:
        state = states[h]
        for b in range(4):
            states_at[h, b] = halves(state)
            if b < 3:
                state = block_decay[h] * state + gained[h, b]
    cotangents = {}
    for at in forward:
        carried = two((q[at], q[at]), states_at[at], ((1,), (0,)))
        output = dot(scores[at], v[at], ((1,), (0,))) + inward[at[0]] * carried
        cotangents[at] = (factor * keep[at[1]] * output).astype(bf16)
    for at in backward:
        scaled = halves(q[at].astype(f32) * inward[at[0]])
        gained[at] = two(scaled, (cotangents[at], cotangents[at]), ((0,), (0,)))
    ends = []
    for h in heads:
        state = gained[h, 3]
        for b in (2, 1, 0):
            states_at[h, b] = halves(state)
            state = block_decay[h] * state + gained[h, b]
        ends.append(state)
    weights, grads = {}, {}
    for at in backward:
        weights[at] = (dot(cotangents[at], v[at], ((1,), (1,))) * decay[at[0]]).astype(bf16)
    for at in backward:
        grad = dot(weights[at], q[at], ((0,), (0,)))
        if at[1] < 3:
            carried = two((v[at], v[at]), states_at[at], ((1,), (1,)))
            grad = grad + outward[at[0]] * carried
        grads[at] = keep[at[1]] * grad
    return grads, ends


def main_body(start, heads, aliased, place, rates, factor_ref, *refs):
    local, refs = refs[: 3 * heads], refs[3 * heads :]
    moved, prompt_ref, refs = refs[:3], refs[3], refs[4 + aliased :]
    outs, prompt_grad_ref = refs[:4], refs[4]
    rows_q, rows_k, rows_v, grads_ref = refs[5:]
    me, length = place[0], place[1]
    row = lax.broadcasted_iota(jnp.int32, (lane, lane), 0)
    for step in range(heads):
        for turn in range(4):
            block = lax.rem(me + 4 - turn, 4)
            if turn == 0:
                q, k, v = (r[...].astype(f32) for r in local[3 * step : 3 * step + 3])
            else:
                q, k, v = (moved[turn - 1][which, step] for which in range(3))
            keep = (row + lane * block < length).astype(f32)
            rows_q[step, block] = q.astype(bf16)
            rows_k[step, block] = (k * keep).astype(bf16)
            rows_v[step, block] = (v * keep).astype(bf16)
    half, steps = lane // 2, range(heads)
    head = residue(me) + 4 * (start + pl.program_id(0) * heads)
    prompts = [
        jnp.concatenate([prompt_ref[2 * step, :half], prompt_ref[2 * step + 1, :half]], 0)
        for step in steps
    ]
    rows = [
        [[r[step, block] for block in range(4)] for r in (rows_q, rows_k, rows_v)]
        for step in steps
    ]
    grads, ends = head_grads(
        [rates[head + 4 * step] for step in steps], factor_ref[0], length, rows, prompts
    )
    for step in steps:
        for block in range(4):
            grads_ref[step, block] = grads[step, block]
        prompt_grad_ref[step] = ends[step]
    for step in range(heads):
        for turn in range(4):
            outs[turn][step] = grads_ref[step, lax.rem(me + turn, 4)]


def main(place, rates, factor, arrays, moved, prompt, so_far, block_len, start, count, heads=2):
    assert block_len == lane
    first, total = start // heads, prompt.shape[0] // 2
    in_specs = [pl.BlockSpec(memory_space=pltpu.SMEM)] * 2

    def column(step):
        return lambda m, place: (0, residue(place[0]) + 4 * (start + m * heads + step))

    def rest(part):
        skipped = 0 if part.shape[1] == count else first
        return lambda m, place: (0, m + skipped, 0, 0)

    in_specs += [
        pl.BlockSpec((block_len, lane), column(step)) for step in range(heads) for _ in arrays
    ]
    in_specs += [pl.BlockSpec((3, heads, block_len, lane), rest(part)) for part in moved]
    in_specs += [
        pl.BlockSpec((2 * heads,) + prompt.shape[1:], lambda m, place: (first + m, 0, 0))
    ]
    args = [place, rates, factor, *(list(arrays) * heads), *moved, prompt]
    aliases = {len(args) + n: n for n in range(len(so_far))}
    in_specs += [pl.BlockSpec(memory_space=pl.ANY)] * len(so_far)
    one = pl.BlockSpec((heads, block_len, lane), lambda m, place: (first + m, 0, 0))
    return pl.pallas_call(
        functools.partial(main_body, start, heads, len(so_far)),
        grid_spec=pltpu.PrefetchScalarGridSpec(
            num_scalar_prefetch=1,
            grid=(count // heads,),
            in_specs=in_specs,
            out_specs=[one] * 5,
            scratch_shapes=[pltpu.VMEM((heads, 4, lane, lane), bf16)] * 3
            + [pltpu.VMEM((heads, 4, lane, lane), f32)],
        ),
        out_shape=[jax.ShapeDtypeStruct((total, block_len, lane), f32)] * 5,
        input_output_aliases=aliases,
        cost_estimate=pl.CostEstimate(
            flops=count * 4 * 15 * 2 * lane**3,
            bytes_accessed=count * lane * lane * 4 * 20,
            transcendentals=0,
        ),
    )(*args, *so_far)


def put_body(heads, place, *refs):
    parts, out = refs[:4], refs[4]
    for turn in range(4):
        owner = residue(lax.rem(place[0] + 4 - turn, 4))
        for step in range(heads):
            column = pl.multiple_of((owner + 4 * step) * lane, lane)
            out[:, pl.ds(column, lane)] = parts[turn][step].astype(bf16)


def put(place, parts, block_len, width, heads=4):
    return pl.pallas_call(
        functools.partial(put_body, heads),
        grid_spec=pltpu.PrefetchScalarGridSpec(
            num_scalar_prefetch=1,
            grid=(parts[0].shape[0] // heads,),
            in_specs=[pl.BlockSpec((heads, block_len, lane), lambda m, place: (m, 0, 0))] * 4,
            out_specs=pl.BlockSpec((block_len, 4 * heads * lane), lambda m, place: (0, m)),
        ),
        out_shape=jax.ShapeDtypeStruct((block_len, width), bf16),
        cost_estimate=pl.CostEstimate(
            flops=0, bytes_accessed=parts[0].size * 24, transcendentals=0
        ),
    )(place, *parts)


def home(ctx, piece):
    return 4 * (2 * (piece // 2) + ctx % 2) + 2 * (ctx // 2) + piece % 2


def shards(queries, keys, values, lengths, rewards, decay_rate, prompt_state):
    block_len, width = queries.shape[2], queries.shape[3]
    arrays = [a.reshape(block_len, width) for a in (queries, keys, values)]
    ctx_index = lax.axis_index("ctx").astype(jnp.int32)
    length, reward = lengths[0, 0], rewards[0, 0]
    place = jnp.stack([ctx_index, length])
    moves = [(home(ctx, slot), 4 * slot + ctx) for slot in range(16) for ctx in range(4)]

    piece = lax.ppermute(prompt_state[0], ("slot", "ctx"), moves)
    rings = [[(i, (i + turn) % 4) for i in range(4)] for turn in range(4)]

    def turned(part, turn):
        return lax.ppermute(part, "ctx", rings[turn])

    piece, sends = lax.optimization_barrier((piece, pack(arrays, block_len)))
    across = turned(sends[0], 2)
    moved = [(turned(sends[n], 1), across, turned(sends[n + 1], 3)) for n in (1, 3)]

    slot_tokens = jnp.full((1, lane), lax.psum(length.astype(f32), "group"))
    scalars = jnp.concatenate(
        [slot_tokens, jnp.full((1, lane), reward), jnp.zeros((6, lane), f32)], 0
    )
    prompt = lax.all_gather(jnp.concatenate([piece, scalars], 0), "slot")
    rows = piece.shape[0]
    token_total = jnp.sum(prompt[:, rows, 0])
    reward_total = jnp.sum(prompt[:, rows + 1, 0])
    slots, groups = lax.axis_size("slot"), lax.axis_size("group")
    advantage = reward - reward_total / slots
    factor = (loss_scale * advantage * (groups * slots) / token_total).reshape(1)

    out = ()
    for start, count, parts in ((0, early, moved[0]), (early, late, moved[1])):
        out = main(
            place, decay_rate, factor, arrays, parts, prompt, out, block_len, start, count
        )
    back = [turned(out[turn], turn) for turn in (1, 2, 3)]
    terms = lax.all_to_all(out[4].reshape(slots, rows, lane), "slot", 0, 0, tiled=True)
    summed = jnp.sum(terms, 0, keepdims=True)
    summed = lax.ppermute(summed, ("slot", "ctx"), [(there, home) for home, there in moves])
    key_grad = put(place, [out[0], *back], block_len, width)
    return (key_grad.reshape(1, 1, block_len, width), summed)


def solution(mesh):
    placed = (
        P("group", "slot", "ctx", None),
        P("group", "slot", "ctx", None),
        P("group", "slot", "ctx", None),
        P("group", "slot"),
        P("group", "slot"),
        P(),
        P("group", ("slot", "ctx"), None),
    )
    return jax.shard_map(
        shards,
        mesh=mesh,
        in_specs=placed,
        out_specs=(P("group", "slot", "ctx", None), P("group", ("slot", "ctx"), None)),
        check_vma=False,
    )
```

```python
import functools

import jax
import jax.numpy as jnp
from jax import lax
from jax.experimental import pallas as pl
from jax.experimental.pallas import tpu as pltpu
from jax.sharding import PartitionSpec as P

loss_scale = 16.0
f32 = jnp.float32
bf16 = jnp.bfloat16
early, late = 6, 2
lane = 128
vmem_bytes = 16 * 1024 * 1024


def dot(a, b, dims):
    return lax.dot_general(a, b, ((dims[0], dims[1]), ((), ())), preferred_element_type=f32)


def halves(x):
    hi = x.astype(bf16)
    return hi, (x - hi.astype(f32)).astype(bf16)


def residue(device):
    return 2 * lax.rem(device, 2) + lax.div(device, 2)


def widen(turn, sources, send, heads):
    owner = residue(lax.rem(lax.axis_index("ctx") + turn, 4))
    for which in range(3):
        for step in range(heads):
            column = pl.multiple_of((owner + 4 * step) * lane, lane)
            send[which, step] = sources[which][:, pl.ds(column, lane)].astype(f32)


def across_body(heads, *refs):
    widen(2, refs[:3], refs[3], heads)


def beside_body(heads, *refs):
    sources, soon, later = refs[:3], refs[3:5], refs[5:7]
    turns = early // heads

    @pl.when(pl.program_id(0) < turns)
    def _():
        widen(1, sources, soon[0], heads)
        widen(3, sources, soon[1], heads)

    @pl.when(pl.program_id(0) >= turns)
    def _():
        widen(1, sources, later[0], heads)
        widen(3, sources, later[1], heads)


def pack(arrays, block_len, beside, heads):
    turns = early // heads
    block = (3, heads, block_len, lane)
    if beside:
        soon = pl.BlockSpec(block, lambda m: (0, lax.min(m, turns - 1), 0, 0))
        later = pl.BlockSpec(block, lambda m: (0, lax.max(m - turns, 0), 0, 0))
        specs, counts, body = [soon, soon, later, later], (early, early, late, late), beside_body
    else:
        specs, counts = [pl.BlockSpec(block, lambda m: (0, m, 0, 0))], (early + late,)
        body = across_body
    return pl.pallas_call(
        functools.partial(body, heads),
        grid=((early + late) // heads,),
        in_specs=[pl.BlockSpec((block_len, 4 * heads * lane), lambda m: (0, m))] * 3,
        out_specs=specs,
        out_shape=[jax.ShapeDtypeStruct((3, count, block_len, lane), f32) for count in counts],
        cost_estimate=pl.CostEstimate(
            flops=0, bytes_accessed=48 * (early + late) * block_len * lane, transcendentals=0
        ),
    )(*arrays)


def head_grads(rates, factor, length, rows, states):
    row = lax.broadcasted_iota(jnp.int32, (lane, lane), 0)
    col = lax.broadcasted_iota(jnp.int32, (lane, lane), 1)
    row_f, offset = row.astype(f32), (row - col).astype(f32)
    keep = [(row + lane * block < length).astype(f32) for block in range(4)]
    heads = range(len(rates))
    decay = [
        jnp.where(offset >= 0.0, jnp.exp(-rate * jnp.maximum(offset, 0.0)), 0.0) for rate in rates
    ]
    inward = [jnp.exp(-(row_f + 1.0) * rate) for rate in rates]
    outward = [jnp.exp(-(lane - 1.0 - row_f) * rate) for rate in rates]
    block_decay = [jnp.exp(jnp.full((lane, lane), -float(lane), f32) * rate) for rate in rates]
    q, k, v = ({(h, b): rows[h][n][b] for h in heads for b in range(4)} for n in range(3))
    forward = [(h, b) for b in range(4) for h in heads]
    backward = forward[::-1]

    def two(a, b, dims):
        a, b = jnp.concatenate(a, dims[0][0]), jnp.concatenate(b, dims[1][0])
        return dot(a, b, dims)

    scores, gained, states_at = {}, {}, {}
    for at in forward:
        scores[at] = (dot(q[at], k[at], ((1,), (1,))) * decay[at[0]]).astype(bf16)
    for at in forward:
        if at[1] < 3:
            scaled = halves(k[at].astype(f32) * outward[at[0]])
            gained[at] = two(scaled, (v[at], v[at]), ((0,), (0,)))
    for h in heads:
        state = states[h]
        for b in range(4):
            states_at[h, b] = halves(state)
            if b < 3:
                state = block_decay[h] * state + gained[h, b]
    cotangents = {}
    for at in forward:
        carried = two((q[at], q[at]), states_at[at], ((1,), (0,)))
        output = dot(scores[at], v[at], ((1,), (0,))) + inward[at[0]] * carried
        cotangents[at] = (factor * keep[at[1]] * output).astype(bf16)
    for at in backward:
        scaled = halves(q[at].astype(f32) * inward[at[0]])
        gained[at] = two(scaled, (cotangents[at], cotangents[at]), ((0,), (0,)))
    ends = []
    for h in heads:
        state = gained[h, 3]
        for b in (2, 1, 0):
            states_at[h, b] = halves(state)
            state = block_decay[h] * state + gained[h, b]
        ends.append(state)
    weights, grads = {}, {}
    for at in backward:
        weights[at] = (dot(cotangents[at], v[at], ((1,), (1,))) * decay[at[0]]).astype(bf16)
    for at in backward:
        grad = dot(weights[at], q[at], ((0,), (0,)))
        if at[1] < 3:
            carried = two((v[at], v[at]), states_at[at], ((1,), (1,)))
            grad = grad + outward[at[0]] * carried
        grads[at] = keep[at[1]] * grad
    return grads, ends


def main_body(start, heads, scale, aliased, place, rates, reward, *refs):
    local, refs = refs[: 3 * heads], refs[3 * heads :]
    moved, prompt_ref, sums_ref, refs = refs[:3], refs[3], refs[4], refs[5 + aliased :]
    sums = jnp.sum(sums_ref[...], 0)
    slots = sums_ref.shape[0]
    factor = scale * (reward[0] - sums[1:2] / slots) / sums[0:1]
    outs, prompt_grad_ref = refs[:4], refs[4]
    rows_q, rows_k, rows_v, grads_ref = refs[5:]
    me, length = place[0], place[1]
    row = lax.broadcasted_iota(jnp.int32, (lane, lane), 0)
    for step in range(heads):
        for turn in range(4):
            block = lax.rem(me + 4 - turn, 4)
            if turn == 0:
                q, k, v = (r[...].astype(f32) for r in local[3 * step : 3 * step + 3])
            else:
                q, k, v = (moved[turn - 1][which, step] for which in range(3))
            keep = (row + lane * block < length).astype(f32)
            rows_q[step, block] = q.astype(bf16)
            rows_k[step, block] = (k * keep).astype(bf16)
            rows_v[step, block] = (v * keep).astype(bf16)
    half, steps = lane // 2, range(heads)
    head = residue(me) + 4 * (start + pl.program_id(0) * heads)
    prompts = [
        jnp.concatenate([prompt_ref[2 * step, :half], prompt_ref[2 * step + 1, :half]], 0)
        for step in steps
    ]
    rows = [
        [[r[step, block] for block in range(4)] for r in (rows_q, rows_k, rows_v)]
        for step in steps
    ]
    grads, ends = head_grads(
        [rates[head + 4 * step] for step in steps], factor, length, rows, prompts
    )
    for step in steps:
        for block in range(4):
            grads_ref[step, block] = grads[step, block]
        prompt_grad_ref[step] = ends[step]
    for step in range(heads):
        for turn in range(4):
            outs[turn][step] = grads_ref[step, lax.rem(me + turn, 4)]


def main(place, rates, reward, scale, arrays, moved, prompt, so_far, block_len, start, count, heads=2):
    assert block_len == lane
    first, total = start // heads, prompt.shape[0] // 2
    in_specs = [pl.BlockSpec(memory_space=pltpu.SMEM)] * 2

    def column(step):
        return lambda m, place: (0, residue(place[0]) + 4 * (start + m * heads + step))

    def rest(part):
        skipped = 0 if part.shape[1] == count else first
        return lambda m, place: (0, m + skipped, 0, 0)

    in_specs += [
        pl.BlockSpec((block_len, lane), column(step)) for step in range(heads) for _ in arrays
    ]
    in_specs += [pl.BlockSpec((3, heads, block_len, lane), rest(part)) for part in moved]
    in_specs += [
        pl.BlockSpec((2 * heads, lane // 2, lane), lambda m, place: (first + m, 0, 0)),
        pl.BlockSpec((prompt.shape[0], 8, lane), lambda m, place: (0, lane // 16, 0)),
    ]
    args = [place, rates, reward, *(list(arrays) * heads), *moved, prompt, prompt]
    aliases = {len(args) + n: n for n in range(len(so_far))}
    in_specs += [pl.BlockSpec(memory_space=pl.ANY)] * len(so_far)
    one = pl.BlockSpec((heads, block_len, lane), lambda m, place: (first + m, 0, 0))
    return pl.pallas_call(
        functools.partial(main_body, start, heads, scale, len(so_far)),
        grid_spec=pltpu.PrefetchScalarGridSpec(
            num_scalar_prefetch=1,
            grid=(count // heads,),
            in_specs=in_specs,
            out_specs=[one] * 5,
            scratch_shapes=[pltpu.VMEM((heads, 4, lane, lane), bf16)] * 3
            + [pltpu.VMEM((heads, 4, lane, lane), f32)],
        ),
        out_shape=[pltpu.HBM((total, block_len, lane), f32)] * 5,
        input_output_aliases=aliases,
        compiler_params=pltpu.CompilerParams(vmem_limit_bytes=vmem_bytes),
        cost_estimate=pl.CostEstimate(
            flops=count * 4 * 15 * 2 * lane**3,
            bytes_accessed=count * lane * lane * 4 * 20,
            transcendentals=0,
        ),
    )(*args, *so_far)


def put_body(heads, place, *refs):
    parts, out = refs[:4], refs[4]
    for turn in range(4):
        owner = residue(lax.rem(place[0] + 4 - turn, 4))
        for step in range(heads):
            column = pl.multiple_of((owner + 4 * step) * lane, lane)
            out[:, pl.ds(column, lane)] = parts[turn][step].astype(bf16)


def put(place, parts, block_len, width, heads=4):
    return pl.pallas_call(
        functools.partial(put_body, heads),
        grid_spec=pltpu.PrefetchScalarGridSpec(
            num_scalar_prefetch=1,
            grid=(parts[0].shape[0] // heads,),
            in_specs=[pl.BlockSpec((heads, block_len, lane), lambda m, place: (m, 0, 0))] * 4,
            out_specs=pl.BlockSpec((block_len, 4 * heads * lane), lambda m, place: (0, m)),
        ),
        out_shape=jax.ShapeDtypeStruct((block_len, width), bf16),
        compiler_params=pltpu.CompilerParams(vmem_limit_bytes=vmem_bytes),
        cost_estimate=pl.CostEstimate(
            flops=0, bytes_accessed=parts[0].size * 24, transcendentals=0
        ),
    )(place, *parts)


def home(ctx, piece):
    return 4 * (2 * (piece // 2) + ctx % 2) + 2 * (ctx // 2) + piece % 2


def shards(queries, keys, values, lengths, rewards, decay_rate, prompt_state):
    block_len, width = queries.shape[2], queries.shape[3]
    arrays = [a.reshape(block_len, width) for a in (queries, keys, values)]
    ctx_index = lax.axis_index("ctx").astype(jnp.int32)
    length, reward = lengths[0, 0], rewards[0, 0]
    place = jnp.stack([ctx_index, length])
    moves = [(home(ctx, slot), 4 * slot + ctx) for slot in range(16) for ctx in range(4)]

    piece = lax.ppermute(prompt_state[0], ("slot", "ctx"), moves)
    rings = [[(i, (i + turn) % 4) for i in range(4)] for turn in range(4)]

    def turned(part, turn):
        return lax.ppermute(part, "ctx", rings[turn])

    piece, (wide,) = lax.optimization_barrier((piece, pack(arrays, block_len, False, 4)))
    across = turned(wide, 2)
    piece, sends = lax.optimization_barrier((piece, pack(arrays, block_len, True, 2)))
    moved = [(turned(sends[n], 1), across, turned(sends[n + 1], 3)) for n in (0, 2)]

    slot_tokens = jnp.full((1, lane), lax.psum(length.astype(f32), "group"))
    scalars = jnp.concatenate(
        [slot_tokens, jnp.full((1, lane), reward), jnp.zeros((6, lane), f32)], 0
    )
    prompt = lax.all_gather(jnp.concatenate([piece, scalars], 0), "slot")
    rows, slots = piece.shape[0], lax.axis_size("slot")
    scale = loss_scale * lax.axis_size("group") * slots

    out = ()
    for start, count, parts in ((0, early, moved[0]), (early, late, moved[1])):
        out = main(
            place, decay_rate, rewards[0], scale, arrays, parts, prompt, out, block_len, start, count
        )
    back = [turned(out[turn], turn) for turn in (1, 2, 3)]
    terms = lax.all_to_all(out[4].reshape(slots, rows, lane), "slot", 0, 0, tiled=True)
    summed = jnp.sum(terms, 0, keepdims=True)
    summed = lax.ppermute(summed, ("slot", "ctx"), [(there, home) for home, there in moves])
    key_grad = put(place, [out[0], *back], block_len, width)
    return (key_grad.reshape(1, 1, block_len, width), summed)


def solution(mesh):
    placed = (
        P("group", "slot", "ctx", None),
        P("group", "slot", "ctx", None),
        P("group", "slot", "ctx", None),
        P("group", "slot"),
        P("group", "slot"),
        P(),
        P("group", ("slot", "ctx"), None),
    )
    return jax.shard_map(
        shards,
        mesh=mesh,
        in_specs=placed,
        out_specs=(P("group", "slot", "ctx", None), P("group", ("slot", "ctx"), None)),
        check_vma=False,
    )
```

```python
import functools

import jax
import jax.numpy as jnp
from jax import lax
from jax.experimental import pallas as pl
from jax.experimental.pallas import tpu as pltpu
from jax.sharding import PartitionSpec as P

loss_scale = 16.0
f32 = jnp.float32
bf16 = jnp.bfloat16
early, late = 6, 2
lane = 128
vmem_bytes = 16 * 1024 * 1024


def dot(a, b, dims):
    return lax.dot_general(a, b, ((dims[0], dims[1]), ((), ())), preferred_element_type=f32)


def halves(x):
    hi = x.astype(bf16)
    return hi, (x - hi.astype(f32)).astype(bf16)


def residue(device):
    return 2 * lax.rem(device, 2) + lax.div(device, 2)


def widen(sources, send):
    for n, source in enumerate(sources):
        send[n % 3, n // 3] = source[...].astype(f32)


def across_body(me, *refs):
    widen(refs[:-1], refs[-1])


def beside_body(me, *refs):
    blocks = len(refs[:-4]) // 2
    right, left, soon, later = refs[:blocks], refs[blocks:-4], refs[-4:-2], refs[-2:]
    turns = early // (blocks // 3)

    @pl.when(pl.program_id(0) < turns)
    def _():
        widen(right, soon[0])
        widen(left, soon[1])

    @pl.when(pl.program_id(0) >= turns)
    def _():
        widen(right, later[0])
        widen(left, later[1])


def pack(me, arrays, block_len, beside, heads):
    turns = early // heads
    block = (3, heads, block_len, lane)

    def column(turn, step):
        return lambda m, me: (0, residue(lax.rem(me[0] + turn, 4)) + 4 * (m * heads + step))

    if beside:
        soon = pl.BlockSpec(block, lambda m, me: (0, lax.min(m, turns - 1), 0, 0))
        later = pl.BlockSpec(block, lambda m, me: (0, lax.max(m - turns, 0), 0, 0))
        specs, counts, body = [soon, soon, later, later], (early, early, late, late), beside_body
    else:
        specs, counts = [pl.BlockSpec(block, lambda m, me: (0, m, 0, 0))], (early + late,)
        body = across_body
    in_specs = [
        pl.BlockSpec((block_len, lane), column(turn, step))
        for turn in ((1, 3) if beside else (2,))
        for step in range(heads)
        for _ in arrays
    ]
    return pl.pallas_call(
        body,
        grid_spec=pltpu.PrefetchScalarGridSpec(
            num_scalar_prefetch=1,
            grid=((early + late) // heads,),
            in_specs=in_specs,
            out_specs=specs,
        ),
        out_shape=[jax.ShapeDtypeStruct((3, count, block_len, lane), f32) for count in counts],
        cost_estimate=pl.CostEstimate(
            flops=0, bytes_accessed=48 * (early + late) * block_len * lane, transcendentals=0
        ),
    )(me, *(list(arrays) * (len(in_specs) // 3)))


def head_grads(rates, factor, length, rows, states):
    row = lax.broadcasted_iota(jnp.int32, (lane, lane), 0)
    col = lax.broadcasted_iota(jnp.int32, (lane, lane), 1)
    row_f, offset = row.astype(f32), (row - col).astype(f32)
    keep = [(row + lane * block < length).astype(f32) for block in range(4)]
    heads = range(len(rates))
    decay = [
        jnp.where(offset >= 0.0, jnp.exp(-rate * jnp.maximum(offset, 0.0)), 0.0) for rate in rates
    ]
    inward = [jnp.exp(-(row_f + 1.0) * rate) for rate in rates]
    outward = [jnp.exp(-(lane - 1.0 - row_f) * rate) for rate in rates]
    block_decay = [jnp.exp(jnp.full((lane, lane), -float(lane), f32) * rate) for rate in rates]
    q, k, v = ({(h, b): rows[h][n][b] for h in heads for b in range(4)} for n in range(3))
    forward = [(h, b) for b in range(4) for h in heads]
    backward = forward[::-1]

    def two(a, b, dims):
        a, b = jnp.concatenate(a, dims[0][0]), jnp.concatenate(b, dims[1][0])
        return dot(a, b, dims)

    scores, gained, states_at = {}, {}, {}
    for at in forward:
        scores[at] = (dot(q[at], k[at], ((1,), (1,))) * decay[at[0]]).astype(bf16)
    for at in forward:
        if at[1] < 3:
            scaled = halves(k[at].astype(f32) * outward[at[0]])
            gained[at] = two(scaled, (v[at], v[at]), ((0,), (0,)))
    for h in heads:
        state = states[h]
        for b in range(4):
            states_at[h, b] = halves(state)
            if b < 3:
                state = block_decay[h] * state + gained[h, b]
    cotangents = {}
    for at in forward:
        carried = two((q[at], q[at]), states_at[at], ((1,), (0,)))
        output = dot(scores[at], v[at], ((1,), (0,))) + inward[at[0]] * carried
        cotangents[at] = (factor * keep[at[1]] * output).astype(bf16)
    for at in backward:
        scaled = halves(q[at].astype(f32) * inward[at[0]])
        gained[at] = two(scaled, (cotangents[at], cotangents[at]), ((0,), (0,)))
    ends = []
    for h in heads:
        state = gained[h, 3]
        for b in (2, 1, 0):
            states_at[h, b] = halves(state)
            state = block_decay[h] * state + gained[h, b]
        ends.append(state)
    weights, grads = {}, {}
    for at in backward:
        weights[at] = (dot(cotangents[at], v[at], ((1,), (1,))) * decay[at[0]]).astype(bf16)
    for at in backward:
        grad = dot(weights[at], q[at], ((0,), (0,)))
        if at[1] < 3:
            carried = two((v[at], v[at]), states_at[at], ((1,), (1,)))
            grad = grad + outward[at[0]] * carried
        grads[at] = keep[at[1]] * grad
    return grads, ends


def main_body(start, heads, scale, aliased, place, rates, reward, *refs):
    local, refs = refs[: 3 * heads], refs[3 * heads :]
    moved, prompt_ref, sums_ref, refs = refs[:3], refs[3], refs[4], refs[5 + aliased :]
    sums = jnp.sum(sums_ref[...], 0)
    slots = sums_ref.shape[0]
    factor = scale * (reward[0] - sums[1:2] / slots) / sums[0:1]
    outs, prompt_grad_ref = refs[:4], refs[4]
    rows_q, rows_k, rows_v, grads_ref = refs[5:]
    me, length = place[0], place[1]
    row = lax.broadcasted_iota(jnp.int32, (lane, lane), 0)
    for step in range(heads):
        for turn in range(4):
            block = lax.rem(me + 4 - turn, 4)
            if turn == 0:
                q, k, v = (r[...].astype(f32) for r in local[3 * step : 3 * step + 3])
            else:
                q, k, v = (moved[turn - 1][which, step] for which in range(3))
            keep = (row + lane * block < length).astype(f32)
            rows_q[step, block] = q.astype(bf16)
            rows_k[step, block] = (k * keep).astype(bf16)
            rows_v[step, block] = (v * keep).astype(bf16)
    half, steps = lane // 2, range(heads)
    head = residue(me) + 4 * (start + pl.program_id(0) * heads)
    prompts = [
        jnp.concatenate([prompt_ref[2 * step, :half], prompt_ref[2 * step + 1, :half]], 0)
        for step in steps
    ]
    rows = [
        [[r[step, block] for block in range(4)] for r in (rows_q, rows_k, rows_v)]
        for step in steps
    ]
    grads, ends = head_grads(
        [rates[head + 4 * step] for step in steps], factor, length, rows, prompts
    )
    for step in steps:
        for block in range(4):
            grads_ref[step, block] = grads[step, block]
        prompt_grad_ref[step] = ends[step]
    for step in range(heads):
        for turn in range(4):
            outs[turn][step] = grads_ref[step, lax.rem(me + turn, 4)]


def main(place, rates, reward, scale, arrays, moved, prompt, so_far, block_len, start, count, heads=2):
    assert block_len == lane
    first, total = start // heads, prompt.shape[0] // 2
    in_specs = [pl.BlockSpec(memory_space=pltpu.SMEM)] * 2

    def column(step):
        return lambda m, place: (0, residue(place[0]) + 4 * (start + m * heads + step))

    def rest(part):
        skipped = 0 if part.shape[1] == count else first
        return lambda m, place: (0, m + skipped, 0, 0)

    in_specs += [
        pl.BlockSpec((block_len, lane), column(step)) for step in range(heads) for _ in arrays
    ]
    in_specs += [pl.BlockSpec((3, heads, block_len, lane), rest(part)) for part in moved]
    in_specs += [
        pl.BlockSpec((2 * heads, lane // 2, lane), lambda m, place: (first + m, 0, 0)),
        pl.BlockSpec((prompt.shape[0], 8, lane), lambda m, place: (0, lane // 16, 0)),
    ]
    args = [place, rates, reward, *(list(arrays) * heads), *moved, prompt, prompt]
    aliases = {len(args) + n: n for n in range(len(so_far))}
    in_specs += [pl.BlockSpec(memory_space=pl.ANY)] * len(so_far)
    one = pl.BlockSpec((heads, block_len, lane), lambda m, place: (first + m, 0, 0))
    return pl.pallas_call(
        functools.partial(main_body, start, heads, scale, len(so_far)),
        grid_spec=pltpu.PrefetchScalarGridSpec(
            num_scalar_prefetch=1,
            grid=(count // heads,),
            in_specs=in_specs,
            out_specs=[one] * 5,
            scratch_shapes=[pltpu.VMEM((heads, 4, lane, lane), bf16)] * 3
            + [pltpu.VMEM((heads, 4, lane, lane), f32)],
        ),
        out_shape=[pltpu.HBM((total, block_len, lane), f32)] * 5,
        input_output_aliases=aliases,
        compiler_params=pltpu.CompilerParams(vmem_limit_bytes=vmem_bytes),
        cost_estimate=pl.CostEstimate(
            flops=count * 4 * 15 * 2 * lane**3,
            bytes_accessed=count * lane * lane * 4 * 20,
            transcendentals=0,
        ),
    )(*args, *so_far)


def put_body(heads, place, *refs):
    parts, out = refs[:4], refs[4]
    for turn in range(4):
        owner = residue(lax.rem(place[0] + 4 - turn, 4))
        for step in range(heads):
            column = pl.multiple_of((owner + 4 * step) * lane, lane)
            out[:, pl.ds(column, lane)] = parts[turn][step].astype(bf16)


def put(place, parts, block_len, width, heads=4):
    return pl.pallas_call(
        functools.partial(put_body, heads),
        grid_spec=pltpu.PrefetchScalarGridSpec(
            num_scalar_prefetch=1,
            grid=(parts[0].shape[0] // heads,),
            in_specs=[pl.BlockSpec((heads, block_len, lane), lambda m, place: (m, 0, 0))] * 4,
            out_specs=pl.BlockSpec((block_len, 4 * heads * lane), lambda m, place: (0, m)),
        ),
        out_shape=jax.ShapeDtypeStruct((block_len, width), bf16),
        compiler_params=pltpu.CompilerParams(vmem_limit_bytes=vmem_bytes),
        cost_estimate=pl.CostEstimate(
            flops=0, bytes_accessed=parts[0].size * 24, transcendentals=0
        ),
    )(place, *parts)


def home(ctx, piece):
    return 4 * (2 * (piece // 2) + ctx % 2) + 2 * (ctx // 2) + piece % 2


def shards(queries, keys, values, lengths, rewards, decay_rate, prompt_state):
    block_len, width = queries.shape[2], queries.shape[3]
    arrays = [a.reshape(block_len, width) for a in (queries, keys, values)]
    ctx_index = lax.axis_index("ctx").astype(jnp.int32)
    length, reward = lengths[0, 0], rewards[0, 0]
    place = jnp.stack([ctx_index, length])
    moves = [(home(ctx, slot), 4 * slot + ctx) for slot in range(16) for ctx in range(4)]

    piece = lax.ppermute(prompt_state[0], ("slot", "ctx"), moves)
    rings = [[(i, (i + turn) % 4) for i in range(4)] for turn in range(4)]

    def turned(part, turn):
        return lax.ppermute(part, "ctx", rings[turn])

    (wide,) = pack(ctx_index.reshape(1), arrays, block_len, False, 4)
    across = turned(wide, 2)
    tokens = jnp.full((1, lane), length.astype(f32))
    piece, sends, tokens = lax.optimization_barrier((piece, pack(ctx_index.reshape(1), arrays, block_len, True, 2), tokens))
    moved = [(turned(sends[n], 1), across, turned(sends[n + 1], 3)) for n in (0, 2)]

    groups = lax.axis_size("group")
    for step in (1, 2, 4):
        tokens = tokens + lax.ppermute(tokens, "group", [(i, i ^ step) for i in range(groups)])
    scalars = jnp.concatenate(
        [tokens, jnp.full((1, lane), reward), jnp.zeros((6, lane), f32)], 0
    )
    prompt = lax.all_gather(jnp.concatenate([piece, scalars], 0), "slot")
    rows, slots = piece.shape[0], lax.axis_size("slot")
    scale = loss_scale * lax.axis_size("group") * slots

    out = ()
    for start, count, parts in ((0, early, moved[0]), (early, late, moved[1])):
        out = main(
            place, decay_rate, rewards[0], scale, arrays, parts, prompt, out, block_len, start, count
        )
    back = [turned(out[turn], turn) for turn in (1, 2, 3)]
    terms = lax.all_to_all(out[4].reshape(slots, rows, lane), "slot", 0, 0, tiled=True)
    summed = jnp.sum(terms, 0, keepdims=True)
    summed = lax.ppermute(summed, ("slot", "ctx"), [(there, home) for home, there in moves])
    key_grad = put(place, [out[0], *back], block_len, width)
    return (key_grad.reshape(1, 1, block_len, width), summed)


def solution(mesh):
    placed = (
        P("group", "slot", "ctx", None),
        P("group", "slot", "ctx", None),
        P("group", "slot", "ctx", None),
        P("group", "slot"),
        P("group", "slot"),
        P(),
        P("group", ("slot", "ctx"), None),
    )
    return jax.shard_map(
        shards,
        mesh=mesh,
        in_specs=placed,
        out_specs=(P("group", "slot", "ctx", None), P("group", ("slot", "ctx"), None)),
        check_vma=False,
    )
```

```python
import functools

import jax
import jax.numpy as jnp
from jax import lax
from jax.experimental import pallas as pl
from jax.experimental.pallas import tpu as pltpu
from jax.sharding import PartitionSpec as P

loss_scale = 16.0
f32 = jnp.float32
bf16 = jnp.bfloat16
early, late = 6, 2
lane = 128
vmem_bytes = 16 * 1024 * 1024


def dot(a, b, dims):
    return lax.dot_general(a, b, ((dims[0], dims[1]), ((), ())), preferred_element_type=f32)


def halves(x):
    hi = x.astype(bf16)
    return hi, (x - hi.astype(f32)).astype(bf16)


def residue(device):
    return 2 * lax.rem(device, 2) + lax.div(device, 2)


def widen(sources, send):
    for n, source in enumerate(sources):
        send[n % 3, n // 3] = source[...].astype(f32)


def across_body(me, *refs):
    widen(refs[:-1], refs[-1])


def beside_body(me, *refs):
    blocks = len(refs[:-4]) // 2
    right, left, soon, later = refs[:blocks], refs[blocks:-4], refs[-4:-2], refs[-2:]
    turns = early // (blocks // 3)

    @pl.when(pl.program_id(0) < turns)
    def _():
        widen(right, soon[0])
        widen(left, soon[1])

    @pl.when(pl.program_id(0) >= turns)
    def _():
        widen(right, later[0])
        widen(left, later[1])


def pack(me, arrays, block_len, beside, heads):
    turns = early // heads
    block = (3, heads, block_len, lane)

    def column(turn, step):
        return lambda m, me: (0, residue(lax.rem(me[0] + turn, 4)) + 4 * (m * heads + step))

    if beside:
        soon = pl.BlockSpec(block, lambda m, me: (0, lax.min(m, turns - 1), 0, 0))
        later = pl.BlockSpec(block, lambda m, me: (0, lax.max(m - turns, 0), 0, 0))
        specs, counts, body = [soon, soon, later, later], (early, early, late, late), beside_body
    else:
        specs, counts = [pl.BlockSpec(block, lambda m, me: (0, m, 0, 0))], (early + late,)
        body = across_body
    in_specs = [
        pl.BlockSpec((block_len, lane), column(turn, step))
        for turn in ((1, 3) if beside else (2,))
        for step in range(heads)
        for _ in arrays
    ]
    return pl.pallas_call(
        body,
        grid_spec=pltpu.PrefetchScalarGridSpec(
            num_scalar_prefetch=1,
            grid=((early + late) // heads,),
            in_specs=in_specs,
            out_specs=specs,
        ),
        out_shape=[jax.ShapeDtypeStruct((3, count, block_len, lane), f32) for count in counts],
        cost_estimate=pl.CostEstimate(
            flops=0, bytes_accessed=48 * (early + late) * block_len * lane, transcendentals=0
        ),
    )(me, *(list(arrays) * (len(in_specs) // 3)))


def head_grads(rates, factor, length, rows, states):
    row = lax.broadcasted_iota(jnp.int32, (lane, lane), 0)
    col = lax.broadcasted_iota(jnp.int32, (lane, lane), 1)
    row_f, offset = row.astype(f32), (row - col).astype(f32)
    keep = [(row + lane * block < length).astype(f32) for block in range(4)]
    heads = range(len(rates))
    decay = [
        jnp.where(offset >= 0.0, jnp.exp(-rate * jnp.maximum(offset, 0.0)), 0.0) for rate in rates
    ]
    inward = [jnp.exp(-(row_f + 1.0) * rate) for rate in rates]
    outward = [jnp.exp(-(lane - 1.0 - row_f) * rate) for rate in rates]
    block_decay = [jnp.exp(jnp.full((lane, lane), -float(lane), f32) * rate) for rate in rates]
    q, k, v = ({(h, b): rows[h][n][b] for h in heads for b in range(4)} for n in range(3))
    forward = [(h, b) for b in range(4) for h in heads]
    backward = forward[::-1]

    def two(a, b, dims):
        a, b = jnp.concatenate(a, dims[0][0]), jnp.concatenate(b, dims[1][0])
        return dot(a, b, dims)

    scores, gained, states_at = {}, {}, {}
    for at in forward:
        scores[at] = (dot(q[at], k[at], ((1,), (1,))) * decay[at[0]]).astype(bf16)
    for at in forward:
        if at[1] < 3:
            scaled = halves(k[at].astype(f32) * outward[at[0]])
            gained[at] = two(scaled, (v[at], v[at]), ((0,), (0,)))
    for h in heads:
        state = states[h]
        for b in range(4):
            states_at[h, b] = halves(state)
            if b < 3:
                state = block_decay[h] * state + gained[h, b]
    cotangents = {}
    for at in forward:
        carried = two((q[at], q[at]), states_at[at], ((1,), (0,)))
        output = dot(scores[at], v[at], ((1,), (0,))) + inward[at[0]] * carried
        cotangents[at] = (factor * keep[at[1]] * output).astype(bf16)
    for at in backward:
        scaled = halves(q[at].astype(f32) * inward[at[0]])
        gained[at] = two(scaled, (cotangents[at], cotangents[at]), ((0,), (0,)))
    ends = []
    for h in heads:
        state = gained[h, 3]
        for b in (2, 1, 0):
            states_at[h, b] = halves(state)
            state = block_decay[h] * state + gained[h, b]
        ends.append(state)
    weights, grads = {}, {}
    for at in backward:
        weights[at] = (dot(cotangents[at], v[at], ((1,), (1,))) * decay[at[0]]).astype(bf16)
    for at in backward:
        grad = dot(weights[at], q[at], ((0,), (0,)))
        if at[1] < 3:
            carried = two((v[at], v[at]), states_at[at], ((1,), (1,)))
            grad = grad + outward[at[0]] * carried
        grads[at] = keep[at[1]] * grad
    return grads, ends


def main_body(start, heads, scale, aliased, place, rates, reward, *refs):
    me, length = place[0], place[1]
    for device in range(4):

        @pl.when(me == device)
        def _(device=device):
            main_at(device, length, start, heads, scale, aliased, rates, reward, *refs)


def main_at(me, length, start, heads, scale, aliased, rates, reward, *refs):
    local, refs = refs[: 3 * heads], refs[3 * heads :]
    moved, prompt_ref, sums_ref, refs = refs[:3], refs[3], refs[4], refs[5 + aliased :]
    sums = jnp.sum(sums_ref[...], 0)
    slots = sums_ref.shape[0]
    factor = scale * (reward[0] - sums[1:2] / slots) / sums[0:1]
    outs, prompt_grad_ref = refs[:4], refs[4]
    row = lax.broadcasted_iota(jnp.int32, (lane, lane), 0)
    half, steps = lane // 2, range(heads)
    rows = []
    for step in steps:
        taken = ([], [], [])
        for block in range(4):
            turn = (me - block) % 4
            if turn == 0:
                q, k, v = (r[...].astype(f32) for r in local[3 * step : 3 * step + 3])
            else:
                q, k, v = (moved[turn - 1][which, step] for which in range(3))
            keep = (row + lane * block < length).astype(f32)
            for rows_of, part in zip(taken, (q, k * keep, v * keep)):
                rows_of.append(part.astype(bf16))
        rows.append(taken)
    head = 2 * (me % 2) + me // 2 + 4 * (start + pl.program_id(0) * heads)
    prompts = [
        jnp.concatenate([prompt_ref[2 * step, :half], prompt_ref[2 * step + 1, :half]], 0)
        for step in steps
    ]
    grads, ends = head_grads(
        [rates[head + 4 * step] for step in steps], factor, length, rows, prompts
    )
    for step in steps:
        for turn in range(4):
            outs[turn][step] = grads[step, (me + turn) % 4]
        prompt_grad_ref[step] = ends[step]


def main(place, rates, reward, scale, arrays, moved, prompt, so_far, block_len, start, count, heads=2):
    assert block_len == lane
    first, total = start // heads, prompt.shape[0] // 2
    in_specs = [pl.BlockSpec(memory_space=pltpu.SMEM)] * 2

    def column(step):
        return lambda m, place: (0, residue(place[0]) + 4 * (start + m * heads + step))

    def rest(part):
        skipped = 0 if part.shape[1] == count else first
        return lambda m, place: (0, m + skipped, 0, 0)

    in_specs += [
        pl.BlockSpec((block_len, lane), column(step)) for step in range(heads) for _ in arrays
    ]
    in_specs += [pl.BlockSpec((3, heads, block_len, lane), rest(part)) for part in moved]
    in_specs += [
        pl.BlockSpec((2 * heads, lane // 2, lane), lambda m, place: (first + m, 0, 0)),
        pl.BlockSpec((prompt.shape[0], 8, lane), lambda m, place: (0, lane // 16, 0)),
    ]
    args = [place, rates, reward, *(list(arrays) * heads), *moved, prompt, prompt]
    aliases = {len(args) + n: n for n in range(len(so_far))}
    in_specs += [pl.BlockSpec(memory_space=pl.ANY)] * len(so_far)
    one = pl.BlockSpec((heads, block_len, lane), lambda m, place: (first + m, 0, 0))
    return pl.pallas_call(
        functools.partial(main_body, start, heads, scale, len(so_far)),
        grid_spec=pltpu.PrefetchScalarGridSpec(
            num_scalar_prefetch=1,
            grid=(count // heads,),
            in_specs=in_specs,
            out_specs=[one] * 5,
        ),
        out_shape=[pltpu.HBM((total, block_len, lane), f32)] * 5,
        input_output_aliases=aliases,
        compiler_params=pltpu.CompilerParams(vmem_limit_bytes=vmem_bytes),
        cost_estimate=pl.CostEstimate(
            flops=count * 4 * 15 * 2 * lane**3,
            bytes_accessed=count * lane * lane * 4 * 20,
            transcendentals=0,
        ),
    )(*args, *so_far)


def put_body(heads, place, *refs):
    parts, out = refs[:4], refs[4]
    for n, turn in enumerate((0, 2, 1, 3)):
        owner = residue(lax.rem(place[0] + 4 - turn, 4))
        for step in range(heads):
            column = pl.multiple_of((owner + 4 * step) * lane, lane)
            out[:, pl.ds(column, lane)] = parts[n][step].astype(bf16)


def put(place, parts, block_len, width, heads=4):
    return pl.pallas_call(
        functools.partial(put_body, heads),
        grid_spec=pltpu.PrefetchScalarGridSpec(
            num_scalar_prefetch=1,
            grid=(parts[0].shape[0] // heads,),
            in_specs=[pl.BlockSpec((heads, block_len, lane), lambda m, place: (m, 0, 0))] * 4,
            out_specs=pl.BlockSpec((block_len, 4 * heads * lane), lambda m, place: (0, m)),
        ),
        out_shape=jax.ShapeDtypeStruct((block_len, width), bf16),
        compiler_params=pltpu.CompilerParams(vmem_limit_bytes=vmem_bytes),
        cost_estimate=pl.CostEstimate(
            flops=0, bytes_accessed=parts[0].size * 24, transcendentals=0
        ),
    )(place, *parts)


def home(ctx, piece):
    return 4 * (2 * (piece // 2) + ctx % 2) + 2 * (ctx // 2) + piece % 2


def shards(queries, keys, values, lengths, rewards, decay_rate, prompt_state):
    block_len, width = queries.shape[2], queries.shape[3]
    arrays = [a.reshape(block_len, width) for a in (queries, keys, values)]
    ctx_index = lax.axis_index("ctx").astype(jnp.int32)
    length, reward = lengths[0, 0], rewards[0, 0]
    place = jnp.stack([ctx_index, length])
    moves = [(home(ctx, slot), 4 * slot + ctx) for slot in range(16) for ctx in range(4)]

    piece = lax.ppermute(prompt_state[0], ("slot", "ctx"), moves)
    rings = [[(i, (i + turn) % 4) for i in range(4)] for turn in range(4)]

    def turned(part, turn):
        return lax.ppermute(part, "ctx", rings[turn])

    (wide,) = pack(ctx_index.reshape(1), arrays, block_len, False, 4)
    across = turned(wide, 2)
    tokens = jnp.full((1, lane), length.astype(f32))
    piece, sends, tokens = lax.optimization_barrier((piece, pack(ctx_index.reshape(1), arrays, block_len, True, 2), tokens))
    moved = [(turned(sends[n], 1), across, turned(sends[n + 1], 3)) for n in (0, 2)]

    groups = lax.axis_size("group")
    for step in (1, 2, 4):
        tokens = tokens + lax.ppermute(tokens, "group", [(i, i ^ step) for i in range(groups)])
    scalars = jnp.concatenate(
        [tokens, jnp.full((1, lane), reward), jnp.zeros((6, lane), f32)], 0
    )
    prompt = lax.all_gather(jnp.concatenate([piece, scalars], 0), "slot")
    rows, slots = piece.shape[0], lax.axis_size("slot")
    scale = loss_scale * lax.axis_size("group") * slots

    out = ()
    for start, count, parts in ((0, early, moved[0]), (early, late, moved[1])):
        out = main(
            place, decay_rate, rewards[0], scale, arrays, parts, prompt, out, block_len, start, count
        )
    back = {turn: turned(out[turn], turn) for turn in (2, 1, 3)}
    terms = lax.all_to_all(out[4].reshape(slots, rows, lane), "slot", 0, 0, tiled=True)
    summed = jnp.sum(terms, 0, keepdims=True)
    summed = lax.ppermute(summed, ("slot", "ctx"), [(there, home) for home, there in moves])
    key_grad = put(place, [out[0], back[2], back[1], back[3]], block_len, width)
    return (key_grad.reshape(1, 1, block_len, width), summed)


def solution(mesh):
    placed = (
        P("group", "slot", "ctx", None),
        P("group", "slot", "ctx", None),
        P("group", "slot", "ctx", None),
        P("group", "slot"),
        P("group", "slot"),
        P(),
        P("group", ("slot", "ctx"), None),
    )
    return jax.shard_map(
        shards,
        mesh=mesh,
        in_specs=placed,
        out_specs=(P("group", "slot", "ctx", None), P("group", ("slot", "ctx"), None)),
        check_vma=False,
    )
```

```python
import functools

import jax
import jax.numpy as jnp
from jax import lax
from jax.experimental import pallas as pl
from jax.experimental.pallas import tpu as pltpu
from jax.sharding import PartitionSpec as P

loss_scale = 16.0
f32 = jnp.float32
bf16 = jnp.bfloat16
early, late = 6, 2
lane = 128
vmem_bytes = 16 * 1024 * 1024


def dot(a, b, dims):
    return lax.dot_general(a, b, ((dims[0], dims[1]), ((), ())), preferred_element_type=f32)


def halves(x):
    hi = x.astype(bf16)
    return hi, (x - hi.astype(f32)).astype(bf16)


def residue(device):
    return 2 * lax.rem(device, 2) + lax.div(device, 2)


def widen(sources, send):
    for n, source in enumerate(sources):
        send[n % 3, n // 3] = source[...].astype(f32)


def across_body(me, *refs):
    widen(refs[:-1], refs[-1])


def beside_body(me, *refs):
    blocks = len(refs[:-4]) // 2
    right, left, soon, later = refs[:blocks], refs[blocks:-4], refs[-4:-2], refs[-2:]
    turns = early // (blocks // 3)

    @pl.when(pl.program_id(0) < turns)
    def _():
        widen(right, soon[0])
        widen(left, soon[1])

    @pl.when(pl.program_id(0) >= turns)
    def _():
        widen(right, later[0])
        widen(left, later[1])


def pack(me, arrays, block_len, beside, heads):
    turns = early // heads
    block = (3, heads, block_len, lane)

    def column(turn, step):
        return lambda m, me: (0, residue(lax.rem(me[0] + turn, 4)) + 4 * (m * heads + step))

    if beside:
        soon = pl.BlockSpec(block, lambda m, me: (0, lax.min(m, turns - 1), 0, 0))
        later = pl.BlockSpec(block, lambda m, me: (0, lax.max(m - turns, 0), 0, 0))
        specs, counts, body = [soon, soon, later, later], (early, early, late, late), beside_body
    else:
        specs, counts = [pl.BlockSpec(block, lambda m, me: (0, m, 0, 0))], (early + late,)
        body = across_body
    in_specs = [
        pl.BlockSpec((block_len, lane), column(turn, step))
        for turn in ((1, 3) if beside else (2,))
        for step in range(heads)
        for _ in arrays
    ]
    return pl.pallas_call(
        body,
        grid_spec=pltpu.PrefetchScalarGridSpec(
            num_scalar_prefetch=1,
            grid=((early + late) // heads,),
            in_specs=in_specs,
            out_specs=specs,
        ),
        out_shape=[jax.ShapeDtypeStruct((3, count, block_len, lane), f32) for count in counts],
        cost_estimate=pl.CostEstimate(
            flops=0, bytes_accessed=48 * (early + late) * block_len * lane, transcendentals=0
        ),
    )(me, *(list(arrays) * (len(in_specs) // 3)))


def head_grads(rates, factor, length, rows, states):
    row = lax.broadcasted_iota(jnp.int32, (lane, lane), 0)
    col = lax.broadcasted_iota(jnp.int32, (lane, lane), 1)
    row_f, offset = row.astype(f32), (row - col).astype(f32)
    keep = [(row + lane * block < length).astype(f32) for block in range(4)]
    heads = range(len(rates))
    decay = [
        jnp.where(offset >= 0.0, jnp.exp(-rate * jnp.maximum(offset, 0.0)), 0.0) for rate in rates
    ]
    inward = [jnp.exp(-(row_f + 1.0) * rate) for rate in rates]
    outward = [jnp.exp(-(lane - 1.0 - row_f) * rate) for rate in rates]
    block_decay = [jnp.exp(jnp.full((lane, lane), -float(lane), f32) * rate) for rate in rates]
    q, k, v = ({(h, b): rows[h][n][b] for h in heads for b in range(4)} for n in range(3))
    forward = [(h, b) for b in range(4) for h in heads]
    backward = forward[::-1]

    def two(a, b, dims):
        a, b = jnp.concatenate(a, dims[0][0]), jnp.concatenate(b, dims[1][0])
        return dot(a, b, dims)

    scores, gained, states_at = {}, {}, {}
    for at in forward:
        scores[at] = (dot(q[at], k[at], ((1,), (1,))) * decay[at[0]]).astype(bf16)
    for at in forward:
        if at[1] < 3:
            scaled = halves(k[at].astype(f32) * outward[at[0]])
            gained[at] = two(scaled, (v[at], v[at]), ((0,), (0,)))
    for h in heads:
        state = states[h]
        for b in range(4):
            states_at[h, b] = halves(state)
            if b < 3:
                state = block_decay[h] * state + gained[h, b]
    cotangents = {}
    for at in forward:
        carried = two((q[at], q[at]), states_at[at], ((1,), (0,)))
        output = dot(scores[at], v[at], ((1,), (0,))) + inward[at[0]] * carried
        cotangents[at] = (factor * keep[at[1]] * output).astype(bf16)
    for at in backward:
        scaled = halves(q[at].astype(f32) * inward[at[0]])
        gained[at] = two(scaled, (cotangents[at], cotangents[at]), ((0,), (0,)))
    ends = []
    for h in heads:
        state = gained[h, 3]
        for b in (2, 1, 0):
            states_at[h, b] = halves(state)
            state = block_decay[h] * state + gained[h, b]
        ends.append(state)
    weights, grads = {}, {}
    for at in backward:
        weights[at] = (dot(cotangents[at], v[at], ((1,), (1,))) * decay[at[0]]).astype(bf16)
    for at in backward:
        grad = dot(weights[at], q[at], ((0,), (0,)))
        if at[1] < 3:
            carried = two((v[at], v[at]), states_at[at], ((1,), (1,)))
            grad = grad + outward[at[0]] * carried
        grads[at] = keep[at[1]] * grad
    return grads, ends


def main_body(start, heads, scale, aliased, place, rates, reward, *refs):
    me, length = place[0], place[1]
    for device in range(4):

        @pl.when(me == device)
        def _(device=device):
            main_at(device, length, start, heads, scale, aliased, rates, reward, *refs)


def main_at(me, length, start, heads, scale, aliased, rates, reward, *refs):
    local, refs = refs[: 3 * heads], refs[3 * heads :]
    moved, prompt_ref, sums_ref, refs = refs[:3], refs[3], refs[4], refs[5 + aliased :]
    sums = jnp.sum(sums_ref[...], 0)
    slots = sums_ref.shape[0]
    factor = scale * (reward[0] - sums[1:2] / slots) / sums[0:1]
    outs, prompt_grad_ref = refs[:4], refs[4]
    row = lax.broadcasted_iota(jnp.int32, (lane, lane), 0)
    half, steps = lane // 2, range(heads)
    rows = []
    for step in steps:
        taken = ([], [], [])
        for block in range(4):
            turn = (me - block) % 4
            if turn == 0:
                q, k, v = (r[...].astype(f32) for r in local[3 * step : 3 * step + 3])
            else:
                q, k, v = (moved[turn - 1][which, step] for which in range(3))
            keep = (row + lane * block < length).astype(f32)
            for rows_of, part in zip(taken, (q, k * keep, v * keep)):
                rows_of.append(part.astype(bf16))
        rows.append(taken)
    head = 2 * (me % 2) + me // 2 + 4 * (start + pl.program_id(0) * heads)
    prompts = [
        jnp.concatenate([prompt_ref[2 * step, :half], prompt_ref[2 * step + 1, :half]], 0)
        for step in steps
    ]
    grads, ends = head_grads(
        [rates[head + 4 * step] for step in steps], factor, length, rows, prompts
    )
    for step in steps:
        for turn in range(4):
            outs[turn][step] = grads[step, (me + turn) % 4].astype(outs[turn].dtype)
        prompt_grad_ref[step] = ends[step]


def main(place, rates, reward, scale, arrays, moved, prompt, so_far, block_len, start, count, heads=2):
    assert block_len == lane
    first, total = start // heads, prompt.shape[0] // 2
    in_specs = [pl.BlockSpec(memory_space=pltpu.SMEM)] * 2

    def column(step):
        return lambda m, place: (0, residue(place[0]) + 4 * (start + m * heads + step))

    def rest(part):
        skipped = 0 if part.shape[1] == count else first
        return lambda m, place: (0, m + skipped, 0, 0)

    in_specs += [
        pl.BlockSpec((block_len, lane), column(step)) for step in range(heads) for _ in arrays
    ]
    in_specs += [pl.BlockSpec((3, heads, block_len, lane), rest(part)) for part in moved]
    in_specs += [
        pl.BlockSpec((2 * heads, lane // 2, lane), lambda m, place: (first + m, 0, 0)),
        pl.BlockSpec((prompt.shape[0], 8, lane), lambda m, place: (0, lane // 16, 0)),
    ]
    args = [place, rates, reward, *(list(arrays) * heads), *moved, prompt, prompt]
    aliases = {len(args) + n: n for n in range(len(so_far))}
    in_specs += [pl.BlockSpec(memory_space=pl.ANY)] * len(so_far)
    one = pl.BlockSpec((heads, block_len, lane), lambda m, place: (first + m, 0, 0))
    return pl.pallas_call(
        functools.partial(main_body, start, heads, scale, len(so_far)),
        grid_spec=pltpu.PrefetchScalarGridSpec(
            num_scalar_prefetch=1,
            grid=(count // heads,),
            in_specs=in_specs,
            out_specs=[one] * 5,
        ),
        out_shape=[
            pltpu.HBM((total, block_len, lane), bf16 if n == 0 else f32) for n in range(5)
        ],
        input_output_aliases=aliases,
        compiler_params=pltpu.CompilerParams(vmem_limit_bytes=vmem_bytes),
        cost_estimate=pl.CostEstimate(
            flops=count * 4 * 15 * 2 * lane**3,
            bytes_accessed=count * lane * lane * 4 * 20,
            transcendentals=0,
        ),
    )(*args, *so_far)


def put_body(heads, place, *refs):
    parts, out = refs[:4], refs[4]
    for n, turn in enumerate((0, 2, 1, 3)):
        owner = residue(lax.rem(place[0] + 4 - turn, 4))
        for step in range(heads):
            column = pl.multiple_of((owner + 4 * step) * lane, lane)
            out[:, pl.ds(column, lane)] = parts[n][step].astype(bf16)


def put(place, parts, block_len, width, heads=4):
    return pl.pallas_call(
        functools.partial(put_body, heads),
        grid_spec=pltpu.PrefetchScalarGridSpec(
            num_scalar_prefetch=1,
            grid=(parts[0].shape[0] // heads,),
            in_specs=[pl.BlockSpec((heads, block_len, lane), lambda m, place: (m, 0, 0))] * 4,
            out_specs=pl.BlockSpec((block_len, 4 * heads * lane), lambda m, place: (0, m)),
        ),
        out_shape=jax.ShapeDtypeStruct((block_len, width), bf16),
        compiler_params=pltpu.CompilerParams(vmem_limit_bytes=vmem_bytes),
        cost_estimate=pl.CostEstimate(
            flops=0, bytes_accessed=parts[0].size * 24, transcendentals=0
        ),
    )(place, *parts)


def home(ctx, piece):
    return 4 * (2 * (piece // 2) + ctx % 2) + 2 * (ctx // 2) + piece % 2


def shards(queries, keys, values, lengths, rewards, decay_rate, prompt_state):
    block_len, width = queries.shape[2], queries.shape[3]
    arrays = [a.reshape(block_len, width) for a in (queries, keys, values)]
    ctx_index = lax.axis_index("ctx").astype(jnp.int32)
    length, reward = lengths[0, 0], rewards[0, 0]
    place = jnp.stack([ctx_index, length])
    moves = [(home(ctx, slot), 4 * slot + ctx) for slot in range(16) for ctx in range(4)]

    piece = lax.ppermute(prompt_state[0], ("slot", "ctx"), moves)
    rings = [[(i, (i + turn) % 4) for i in range(4)] for turn in range(4)]

    def turned(part, turn):
        return lax.ppermute(part, "ctx", rings[turn])

    (wide,) = pack(ctx_index.reshape(1), arrays, block_len, False, 4)
    across = turned(wide, 2)
    tokens = jnp.full((1, lane), length.astype(f32))
    piece, sends, tokens = lax.optimization_barrier((piece, pack(ctx_index.reshape(1), arrays, block_len, True, 2), tokens))
    moved = [(turned(sends[n], 1), across, turned(sends[n + 1], 3)) for n in (0, 2)]

    groups = lax.axis_size("group")
    for step in (1, 2, 4):
        tokens = tokens + lax.ppermute(tokens, "group", [(i, i ^ step) for i in range(groups)])
    scalars = jnp.concatenate(
        [tokens, jnp.full((1, lane), reward), jnp.zeros((6, lane), f32)], 0
    )
    prompt = lax.all_gather(jnp.concatenate([piece, scalars], 0), "slot")
    rows, slots = piece.shape[0], lax.axis_size("slot")
    scale = loss_scale * lax.axis_size("group") * slots

    out = ()
    for start, count, parts in ((0, early, moved[0]), (early, late, moved[1])):
        out = main(
            place, decay_rate, rewards[0], scale, arrays, parts, prompt, out, block_len, start, count
        )
    back = {turn: turned(out[turn], turn) for turn in (2, 1, 3)}
    terms = lax.all_to_all(out[4].reshape(slots, rows, lane), "slot", 0, 0, tiled=True)
    summed = jnp.sum(terms, 0, keepdims=True)
    summed = lax.ppermute(summed, ("slot", "ctx"), [(there, home) for home, there in moves])
    key_grad = put(place, [out[0], back[2], back[1], back[3]], block_len, width)
    return (key_grad.reshape(1, 1, block_len, width), summed)


def solution(mesh):
    placed = (
        P("group", "slot", "ctx", None),
        P("group", "slot", "ctx", None),
        P("group", "slot", "ctx", None),
        P("group", "slot"),
        P("group", "slot"),
        P(),
        P("group", ("slot", "ctx"), None),
    )
    return jax.shard_map(
        shards,
        mesh=mesh,
        in_specs=placed,
        out_specs=(P("group", "slot", "ctx", None), P("group", ("slot", "ctx"), None)),
        check_vma=False,
    )
```
